128 devices in a mesh: row: 16 (over z, y), col: 8 (over x, core).
Axes of the slice: x: 4, y: 4, z: 4, core: 2. Of those that a mesh axis runs over, the one named last changes fastest.
Arguments:
- tractions: float32 [3, 512, 32768], P(None, None, ('row', 'col')), may hold values from -1 to 1
- log_state: float32 [512, 32768], P(None, ('row', 'col')), may hold values from -0.5 to 1
- rate_coef: float32 [32768], P(('row', 'col')), may hold values from 0.8 to 1.6
- state_coef: float32 [32768], P(('row', 'col')), may hold values from 0.2 to 0.8
- normal_stress: float32 [32768], P(('row', 'col')), may hold values from 0.5 to 4
- inv_length: float32 [32768], P(('row', 'col')), may hold values from 0.5 to 2
- near_blocks: bfloat16 [128, 3, 3, 2, 256, 256], P(('row', 'col'))
- far_right: bfloat16 [128, 128, 2, 32, 256], P('row', 'col'), may hold values from -0.25 to 0.25
- far_left: bfloat16 [128, 128, 3, 32, 256], P(('row', 'col')), may hold values from -0.25 to 0.25
- ranks: int32 [128, 128], P('row', 'col'), may hold values from 13 to 32, as said below
Outputs:
- new_tractions: float32 [3, 512, 32768], P(None, None, ('row', 'col'))
- new_state: float32 [512, 32768], P(None, ('row', 'col'))
The draws below stay inside these ranges and needn't reach their ends.
Inputs may be any that keep to these rules, and one draw needn't show every extreme that they name: ranks[a, b] rank slots of lattice block (a, b) are used.
All inputs are finite; a program needn't handle non-finite values.
Results may differ from the reference program's by a relative error of at most 0.0003.
Values may be sent and summed in bfloat16 or wider, within the bound.
No kernel may reach another device: no remote copies, remote signals or barrier semaphores. Data moves between devices by JAX's collectives and lax.ppermute only.
A program may use at most 128 MiB of HBM per device.

```python
import math
import jax
import jax.numpy as jnp
from jax import lax

BLOCK = 256
RMAX = 32
ENS = 512
NB = 128
CELLS = 32768
GROUP = 16
STRIDE = 8


def draw_near_blocks(key, part):
    key = jax.random.fold_in(key, 5)
    first_key, second_key = jax.random.split(key)
    shape_all = (NB, 3, 3, 2, BLOCK, BLOCK)
    values = jax.random.normal(first_key, shape_all, jnp.float32)
    values = values * (1.0 / math.sqrt(6.0 * BLOCK))
    self_terms = jax.random.uniform(second_key, (NB, 1, 1, 1, BLOCK, 1), jnp.float32, 1.5, 3.0)
    center_band = jnp.arange(3).reshape(1, 3, 1, 1, 1, 1) == 1
    matched = jnp.arange(3).reshape(1, 1, 3, 1, 1, 1) == jnp.arange(2).reshape(1, 1, 1, 2, 1, 1)
    diagonal = jnp.arange(BLOCK).reshape(1, 1, 1, 1, BLOCK, 1) == jnp.arange(BLOCK).reshape(1, 1, 1, 1, 1, BLOCK)
    values = values - jnp.where(center_band & matched & diagonal, self_terms, 0.0)
    return values.astype(jnp.bfloat16)


def draw_ranks(key, part):
    key = jax.random.fold_in(key, 9)
    level_key, rank_key = jax.random.split(key)
    levels = jax.random.randint(level_key, (NB, 1), 0, 16)
    rank_caps = jnp.where(levels == 0, 4, 3 + levels % 2) * (RMAX // 4)
    half_caps = rank_caps // 2
    uniform_bits = jax.random.randint(rank_key, (NB, NB), 0, 1048576)
    rank_draws = rank_caps - jnp.right_shift(uniform_bits * half_caps, 20)
    corner_cell = (jnp.arange(NB)[:, None] == 0) & (jnp.arange(NB)[None, :] == 0)
    return jnp.where(corner_cell, RMAX, rank_draws).astype(jnp.int32)


def level_of(key, shape, pieces, smallest, top_value):
    level = 1.0
    for dim, parts in pieces:
        steps = jax.random.uniform(jax.random.fold_in(jax.random.fold_in(key, 6), dim), (parts,), jnp.float32, smallest / len(pieces), top_value / len(pieces))
        level = level * jnp.repeat(jnp.exp(steps), shape[dim] // parts).reshape((-1,) + (1,) * (len(shape) - 1 - dim))
    return level


def centred(rng, dims, scale, bound, shards=(), held_as=jnp.bfloat16):
    factor_of = level_of(rng, dims, shards, -0.22, 0.18) if shards else 1.0
    values = jax.random.normal(rng, dims, jnp.float32) * scale * factor_of
    return jnp.minimum(jnp.maximum(values, -bound), bound).astype(held_as)


def setup_inputs(seed: int = 0) -> dict:
    key_of = jax.random.split(jax.random.key(seed), 11)
    tractions = jnp.clip(jax.random.uniform(key_of[0], (3, ENS, CELLS), jnp.float32, -1.0, 1.0) * level_of(key_of[0], (3, ENS, CELLS), ((2, 128),), -0.4, 0.0), -1.0, 1.0)
    log_state = jnp.clip(-0.5 + 1.5 * jax.random.uniform(key_of[1], (ENS, CELLS), jnp.float32) ** level_of(key_of[1], (ENS, CELLS), ((1, 128),), -0.2, 0.2), -0.5, 1.0)
    rate_coef = jnp.clip(jnp.exp(math.log(1.6) - 0.6931472 * jax.random.uniform(key_of[2], (CELLS,), jnp.float32) ** level_of(key_of[2], (CELLS,), ((0, 128),), -0.2, 0.2)), 0.8, 1.6)
    state_coef = jnp.clip(jnp.exp(math.log(0.8) - 1.3862944 * jax.random.uniform(key_of[3], (CELLS,), jnp.float32) ** level_of(key_of[3], (CELLS,), ((0, 128),), -0.2, 0.2)), 0.2, 0.8)
    normal_stress = jnp.clip(jnp.exp(math.log(4.0) - 2.0794415 * jax.random.uniform(key_of[4], (CELLS,), jnp.float32) ** level_of(key_of[4], (CELLS,), ((0, 128),), -0.2, 0.2)), 0.5, 4.0)
    inv_length = jnp.clip(jnp.exp(math.log(2.0) - 1.3862944 * jax.random.uniform(key_of[5], (CELLS,), jnp.float32) ** level_of(key_of[5], (CELLS,), ((0, 128),), -0.2, 0.2)), 0.5, 2.0)
    near_blocks = draw_near_blocks(jax.random.fold_in(key_of[10], 71), 0)
    far_right = centred(key_of[7], (NB, NB, 2, RMAX, BLOCK), (2 * BLOCK) ** -0.5, 0.25, ((0, 16), (1, 8)))
    far_left = centred(key_of[8], (NB, NB, 3, RMAX, BLOCK), (NB * RMAX // 8) ** -0.5, 0.25, ((0, 128),))
    ranks = draw_ranks(jax.random.fold_in(key_of[10], 71), 0)
    return {"tractions": tractions, "log_state": log_state, "rate_coef": rate_coef, "state_coef": state_coef, "normal_stress": normal_stress, "inv_length": inv_length, "near_blocks": near_blocks, "far_right": far_right, "far_left": far_left, "ranks": ranks}


time_step = 0.03

def friction_slip(traction, log_value, rate_coef, state_coef, normal_stress):
    effective = jnp.maximum(normal_stress - traction[2], 1.0)
    scaled = rate_coef * effective
    shear_size = jnp.sqrt(traction[0] * traction[0] + traction[1] * traction[1])
    stress_ratio = shear_size / scaled
    amplitude = 2.0 * jnp.exp(-state_coef * log_value / rate_coef) * jnp.sinh(stress_ratio)
    factor = amplitude / (scaled * jnp.maximum(stress_ratio, 1.0))
    slip_rates = jnp.stack([factor * traction[0], factor * traction[1]]).astype(jnp.bfloat16)
    slip_speed = amplitude * jnp.minimum(stress_ratio, 1.0)
    return (slip_rates, slip_speed)

def fault_rates(traction, log_value, rate_coef, state_coef, normal_stress, inv_length, near_blocks, far_right, far_left, ranks):
    slip_rates, slip_speed = friction_slip(traction, log_value, rate_coef, state_coef, normal_stress)
    blocks = slip_rates.astype(jnp.float32).reshape(2, ENS, NB, BLOCK)
    lattice = jnp.transpose(blocks.reshape(2, ENS, GROUP, STRIDE, BLOCK), (3, 2, 0, 1, 4)).reshape(NB, 2, ENS, BLOCK)
    padded = jnp.pad(blocks, ((0, 0), (0, 0), (1, 1), (0, 0)))
    neighbours = jnp.stack([padded[:, :, offset:offset + NB] for offset in range(3)])
    neighbours = jnp.transpose(neighbours, (3, 0, 1, 2, 4))
    positions = jnp.arange(NB)
    column_block = positions % GROUP * STRIDE + positions // GROUP
    rank_slots = jnp.arange(RMAX)

    def one_row(inputs):
        row_block, near_block, around, right_factors, left_factors, rank_row = inputs
        products = jnp.einsum('bsrp,bsep->bre', right_factors.astype(jnp.float32), lattice)
        active = (rank_slots[None, :] < rank_row[:, None]) & (jnp.abs(row_block - column_block) >= 2)[:, None]
        coefficients = jnp.where(active[:, :, None], products, 0.0).astype(jnp.bfloat16)
        far_part = jnp.einsum('bcrp,bre->cep', left_factors.astype(jnp.float32), coefficients.astype(jnp.float32))
        near_part = jnp.einsum('kcspq,kseq->cep', near_block.astype(jnp.float32), around)
        return far_part + near_part
    row_rates = lax.map(one_row, (positions, near_blocks, neighbours, far_right, far_left, ranks))
    traction_rates = jnp.transpose(row_rates, (1, 2, 0, 3)).reshape(3, ENS, NB * BLOCK)
    state_rates = (jnp.exp(-log_value) - slip_speed) * inv_length
    return (traction_rates, state_rates)

def reference(tractions, log_state, rate_coef, state_coef, normal_stress, inv_length, near_blocks, far_right, far_left, ranks):
    fixed_args = (rate_coef, state_coef, normal_stress, inv_length, near_blocks, far_right, far_left, ranks)
    first_rates, first_state = fault_rates(tractions, log_state, *fixed_args)
    middle = tractions + time_step * first_rates
    middle_state = log_state + time_step * first_state
    second_rates, second_state = fault_rates(middle, middle_state, *fixed_args)
    new_tractions = tractions + 0.5 * time_step * (first_rates + second_rates)
    new_state = log_state + 0.5 * time_step * (first_state + second_state)
    return (new_tractions, new_state)
```

```python
import functools

import jax
import jax.numpy as jnp
from jax import lax
from jax.experimental import pallas as pl
from jax.experimental.pallas import tpu as pltpu
from jax.sharding import PartitionSpec as P

time_step = 0.03
SIDE = 4
CORES = 2
OFFSETS = (0, 1, 3, 2)
VMEM = 40 * 2**20
NT = (((1,), (1,)), ((), ()))


def friction_slip(traction, log_value, rate_coef, state_coef, normal_stress):
    effective = jnp.maximum(normal_stress - traction[2], 1.0)
    scaled = rate_coef * effective
    shear_size = jnp.sqrt(traction[0] * traction[0] + traction[1] * traction[1])
    stress_ratio = shear_size / scaled
    amplitude = 2.0 * jnp.exp(-state_coef * log_value / rate_coef) * jnp.sinh(stress_ratio)
    factor = amplitude / (scaled * jnp.maximum(stress_ratio, 1.0))
    slip_rates = jnp.stack([factor * traction[0], factor * traction[1]]).astype(jnp.bfloat16)
    slip_speed = amplitude * jnp.minimum(stress_ratio, 1.0)
    return (slip_rates, slip_speed)


def from_zy(cells, dz, dy):
    pairs = []
    for i in range(SIDE * SIDE):
        z, y = divmod(i, SIDE)
        pairs.append((((z + dz) % SIDE) * SIDE + (y + dy) % SIDE, i))
    return lax.ppermute(cells, "row", pairs)


def to_xc(values, dx, dc):
    pairs = []
    for i in range(SIDE * CORES):
        x, c = divmod(i, CORES)
        pairs.append((i, ((x + dx) % SIDE) * CORES + (c + dc) % CORES))
    return lax.ppermute(values, "col", pairs)


def beside(cells, step):
    count = lax.axis_size("row") * lax.axis_size("col")
    pairs = [(i, i - step) for i in range(count) if 0 <= i - step < count]
    return lax.ppermute(cells, ("row", "col"), pairs)


def coefficient_kernel(groups, rows, a_index, b_index, rank_ref, *refs):
    count = 2 * groups
    x_refs, r_refs, outs = refs[:count], refs[count : 2 * count], refs[2 * count :]
    step = pl.program_id(0)
    steps = pl.num_programs(0)
    width = r_refs[0].shape[3]
    for k in range(count):
        total = None
        for s in range(2):
            weights = jnp.concatenate([r_refs[k][a_index[i], 0, s] for i in range(rows)], axis=0)
            part = lax.dot_general(weights, x_refs[k][0, s], NT, preferred_element_type=jnp.float32)
            total = part if total is None else total + part
        b = b_index[k * steps + step]
        slot = lax.broadcasted_iota(jnp.int32, (width, total.shape[1]), 0)
        for i in range(rows):
            used = rank_ref[a_index[i], b]
            block = total[i * width : (i + 1) * width]
            outs[i][k // groups, k % groups, 0] = jnp.where(slot < used, block, 0.0).astype(jnp.bfloat16)


def coefficients_of(pieces, b_index, a_index, used, far_right):
    groups = len(pieces[0])
    n, _, members, cells = pieces[0][0].shape
    rows, _, _, width, _ = far_right.shape
    x_spec = pl.BlockSpec((1, 2, members, cells), lambda j, *_: (j, 0, 0, 0))
    r_specs = [
        pl.BlockSpec((rows, 1, 2, width, cells), lambda j, a, b, u, k=k: (0, b[k * n + j], 0, 0, 0))
        for k in range(2 * groups)
    ]
    out = jax.ShapeDtypeStruct((2, groups, n, width, members), jnp.bfloat16)
    out_spec = pl.BlockSpec((2, groups, 1, width, members), lambda j, *_: (0, 0, j, 0, 0))
    flops = 2 * 2 * groups * n * rows * width * 2 * cells * members
    return pl.pallas_call(
        functools.partial(coefficient_kernel, groups, rows),
        grid_spec=pltpu.PrefetchScalarGridSpec(
            num_scalar_prefetch=3,
            grid=(n,),
            in_specs=[x_spec] * (2 * groups) + r_specs,
            out_specs=[out_spec] * rows,
        ),
        out_shape=[out] * rows,
        compiler_params=pltpu.CompilerParams(vmem_limit_bytes=VMEM),
        cost_estimate=pl.CostEstimate(flops=flops, bytes_accessed=flops // 256, transcendentals=0),
        name="coefficients",
    )(a_index, b_index, used, *pieces[0], *pieces[1], *[far_right] * (2 * groups))


def reorder_kernel(index, *refs):
    parts, out = refs[:-1], refs[-1]
    width = parts[0].shape[2]
    for j, part in enumerate(parts):
        for c in range(out.shape[0]):
            out[c, j * width : (j + 1) * width] = part[0, c]


def reordered(far_left, index, batch=8):
    count, sides, width, cells = far_left.shape
    specs = [
        pl.BlockSpec((1, sides, width, cells), lambda g, idx, j=j: (idx[g * batch + j], 0, 0, 0))
        for j in range(batch)
    ]
    return pl.pallas_call(
        reorder_kernel,
        grid_spec=pltpu.PrefetchScalarGridSpec(
            num_scalar_prefetch=1,
            grid=(count // batch,),
            in_specs=specs,
            out_specs=pl.BlockSpec((sides, batch * width, cells), lambda g, idx: (0, g, 0)),
        ),
        out_shape=jax.ShapeDtypeStruct((sides, count * width, cells), far_left.dtype),
        compiler_params=pltpu.CompilerParams(vmem_limit_bytes=VMEM),
        cost_estimate=pl.CostEstimate(flops=0, bytes_accessed=2 * far_left.size * 2, transcendentals=0),
        name="reorder",
    )(index, *[far_left] * batch)


def far_kernel(sources, seeded, *refs):
    coefs = refs[:sources]
    weights = refs[sources : sources + 2]
    before = refs[sources + 2] if seeded else None
    out, turned = refs[-2], refs[-1]
    half, side = pl.program_id(0), pl.program_id(1)

    @pl.when(side == 0)
    def _():
        for i, coef in enumerate(coefs):
            groups, n, width, members = coef.shape[1:]
            depth = groups * n * width
            block = coef[half].reshape(depth, members)
            turned[:, i * depth : (i + 1) * depth] = block.astype(jnp.float32).T.astype(jnp.bfloat16)

    for h in range(2):

        @pl.when(half == h)
        def _():
            value = jnp.dot(turned[...], weights[h][0], preferred_element_type=jnp.float32)
            if seeded:
                value = value + before[0]
            out[0] = value


def far_part(coefs, weights, place, before):
    sources = len(coefs)
    _, groups, n, width, members = coefs[0].shape
    depth = sources * groups * n * width
    sides, _, cells = weights[0].shape
    whole = pl.BlockSpec(coefs[0].shape, lambda h, c: (0, 0, 0, 0, 0))
    out_spec = pl.BlockSpec((1, members, cells), lambda h, c: (c, h, 0))
    w_spec = [
        pl.BlockSpec((1, depth, cells), lambda h, c: (jnp.where(h == 0, c, sides - 1), place, 0)),
        pl.BlockSpec((1, depth, cells), lambda h, c: (jnp.where(h == 1, c, 0), place, 0)),
    ]
    seeded = before is not None
    flops = 2 * 2 * sides * depth * cells * members
    return pl.pallas_call(
        functools.partial(far_kernel, sources, seeded),
        grid=(2, sides),
        in_specs=[whole] * sources + w_spec + ([out_spec] if seeded else []),
        out_specs=out_spec,
        out_shape=jax.ShapeDtypeStruct((sides, 2 * members, cells), jnp.float32),
        scratch_shapes=[pltpu.VMEM((members, depth), jnp.bfloat16)],
        compiler_params=pltpu.CompilerParams(vmem_limit_bytes=VMEM),
        cost_estimate=pl.CostEstimate(flops=flops, bytes_accessed=flops // 256, transcendentals=0),
        name="far",
    )(*coefs, *weights, *([before] if seeded else []))


def near_kernel(x0, x1, x2, weights, out):
    total = None
    for k, x in enumerate((x0, x1, x2)):
        for s in range(2):
            part = lax.dot_general(x[s], weights[k, 0, s], NT, preferred_element_type=jnp.float32)
            total = part if total is None else total + part
    out[0] = total


def near_part(slabs, near_blocks):
    _, members, cells = slabs[0].shape
    sides = near_blocks.shape[1]
    whole = pl.BlockSpec(slabs[0].shape, lambda c: (0, 0, 0))
    flops = 2 * 6 * sides * members * cells * cells
    return pl.pallas_call(
        near_kernel,
        grid=(sides,),
        in_specs=[whole] * 3 + [pl.BlockSpec((3, 1, 2, cells, cells), lambda c: (0, c, 0, 0, 0))],
        out_specs=pl.BlockSpec((1, members, cells), lambda c: (c, 0, 0)),
        out_shape=jax.ShapeDtypeStruct((sides, members, cells), jnp.float32),
        compiler_params=pltpu.CompilerParams(vmem_limit_bytes=VMEM),
        cost_estimate=pl.CostEstimate(flops=flops, bytes_accessed=flops // 256, transcendentals=0),
        name="near",
    )(*slabs, near_blocks)


def on_device(
    tractions, log_state, rate_coef, state_coef, normal_stress, inv_length,
    near_blocks, far_right, far_left, ranks,
):
    row, col = lax.axis_index("row"), lax.axis_index("col")
    col_count = lax.axis_size("col")
    z, y = row // SIDE, row % SIDE
    x, c = col // CORES, col % CORES
    tile_rows, tile_cols = far_right.shape[:2]

    targets = [(dx, dc) for dx in OFFSETS for dc in range(CORES)]
    a_index = jnp.stack([((x + dx) % SIDE) * CORES + (c + dc) % CORES for dx, dc in targets])
    origin = [((x - dx) % SIDE) * CORES + (c + dc) % CORES for dx, dc in targets]
    place = lambda dz, dy: ((z + dz) % SIDE) * SIDE + (y + dy) % SIDE
    outer = [[0], [1, 3], [2]]
    columns = [
        [[place(d, o) for o in chunk for d in OFFSETS] for chunk in outer],
        [[place(o, d) for o in chunk for d in OFFSETS] for chunk in outer],
    ]
    block_row = row * tile_rows + jnp.arange(tile_rows, dtype=jnp.int32)
    block_col = jnp.arange(tile_cols, dtype=jnp.int32) * col_count + col
    near = jnp.abs(block_row[:, None] - block_col[None, :]) < 2
    used = jnp.where(near, 0, ranks)
    b_index = [jnp.stack(columns[0][k] + columns[1][k]) for k in range(3)]
    left = [
        reordered(far_left[0], jnp.stack([o * tile_cols + b for k in (1, 0, 2) for o in origin for b in columns[h][k]]))
        for h in range(2)
    ]
    def exchange(pieces, k):
        sent = coefficients_of(pieces, b_index[k], a_index, used, far_right)
        return [v if t == (0, 0) else to_xc(v, *t) for v, t in zip(sent, targets)]

    def fault_rates(traction_now, state_now):
        slip_rates, slip_speed = friction_slip(
            traction_now, state_now, rate_coef, state_coef, normal_stress
        )
        members = slip_rates.shape[1]
        own = [slip_rates[:, : members // 2], slip_rates[:, members // 2 :]]
        move = [
            [lambda v, d: from_zy(v, d, 0), lambda v, d: from_zy(v, 0, d)],
            [lambda v, d: from_zy(v, 0, d), lambda v, d: from_zy(v, d, 0)],
        ]
        lines = [
            jnp.stack([own[h]] + [move[h][0](own[h], d) for d in OFFSETS[1:]]) for h in range(2)
        ]
        after = [move[h][1](lines[h], 1) for h in range(2)]
        ahead = [move[h][1](lines[h], -1) for h in range(2)]
        middle = len(OFFSETS) // 2
        opposite = [
            [move[h][1](after[h][:middle], 1), move[h][1](ahead[h][middle:], -1)] for h in range(2)
        ]
        slabs = [beside(slip_rates, -1), slip_rates, beside(slip_rates, 1)]
        first = exchange([[lines[0]], [lines[1]]], 0)
        second = exchange([[after[0], ahead[0]], [after[1], ahead[1]]], 1)
        third = exchange(opposite, 2)
        near_rates = near_part(slabs, near_blocks[0])
        rates = far_part(first, left, 2, near_rates)
        rates = far_part(second, left, 0, rates)
        rates = far_part(third, left, 3, rates)
        state_rates = (jnp.exp(-state_now) - slip_speed) * inv_length
        return (rates, state_rates)

    first_rates, first_state = fault_rates(tractions, log_state)
    middle = tractions + time_step * first_rates
    middle_state = log_state + time_step * first_state
    second_rates, second_state = fault_rates(middle, middle_state)
    new_tractions = tractions + 0.5 * time_step * (first_rates + second_rates)
    new_state = log_state + 0.5 * time_step * (first_state + second_state)
    return (new_tractions, new_state)


def solution(mesh):
    placed = (
        P(None, None, ("row", "col")),
        P(None, ("row", "col")),
        P(("row", "col")),
        P(("row", "col")),
        P(("row", "col")),
        P(("row", "col")),
        P(("row", "col"), None, None, None, None, None),
        P("row", "col", None, None, None),
        P(("row", "col"), None, None, None, None),
        P("row", "col"),
    )
    return jax.shard_map(
        on_device,
        mesh=mesh,
        in_specs=placed,
        out_specs=(P(None, None, ("row", "col")), P(None, ("row", "col"))),
        check_vma=False,
    )
```

```python
import functools
import math

import jax
import jax.numpy as jnp
from jax import lax
from jax.experimental import pallas as pl
from jax.experimental.pallas import tpu as pltpu
from jax.sharding import Mesh
from jax.sharding import PartitionSpec as P

time_step = 0.03
PARTS = 2
SIDE = 4
CORES = 2
OFFSETS = (0, 1, 3, 2)
ALL = ("z", "y", "x", "core")
VMEM = 60 * 2**20
ANY = pl.BlockSpec(memory_space=pl.ANY)
NT = (((1,), (1,)), ((), ()))


def sinh(x):
    small = x * x
    series = x * (1.0 + small * (1.0 / 6 + small * (1.0 / 120 + small * (1.0 / 5040))))
    exact = jnp.exp(x - math.log(2.0)) - jnp.exp(-x - math.log(2.0))
    return jnp.where(x < 0.35, series, exact)


def friction_slip(traction, log_value, rate_coef, state_coef, normal_stress):
    effective = jnp.maximum(normal_stress - traction[2], 1.0)
    scaled = rate_coef * effective
    shear_size = jnp.sqrt(traction[0] * traction[0] + traction[1] * traction[1])
    stress_ratio = shear_size / scaled
    amplitude = 2.0 * jnp.exp(-state_coef * log_value / rate_coef) * sinh(stress_ratio)
    factor = amplitude / (scaled * jnp.maximum(stress_ratio, 1.0))
    slip_rates = [(factor * traction[s]).astype(jnp.bfloat16) for s in range(2)]
    slip_speed = amplitude * jnp.minimum(stress_ratio, 1.0)
    return (slip_rates, slip_speed)


def beside(slabs, step):
    count = SIDE**3 * CORES
    pairs = [(i, i - step) for i in range(count) if 0 <= i - step < count]
    return lax.ppermute(slabs, ALL, pairs)


def from_z(slabs, dz):
    return lax.ppermute(slabs, "z", [((i + dz) % SIDE, i) for i in range(SIDE)])


def whole(v):
    return pl.BlockSpec(v.shape, lambda *_: (0,) * len(v.shape))


def call(kernel, name, grid, in_specs, out_specs, out_shape, args, flops, scratch=(), aliases=None):
    return pl.pallas_call(
        kernel,
        grid=grid,
        in_specs=in_specs,
        out_specs=out_specs,
        out_shape=out_shape,
        scratch_shapes=list(scratch),
        input_output_aliases=aliases or {},
        compiler_params=pltpu.CompilerParams(vmem_limit_bytes=VMEM),
        cost_estimate=pl.CostEstimate(flops=flops, bytes_accessed=8 * 2**20, transcendentals=0),
        name=name,
    )(*args)


def mask_kernel(used, right, out):
    rows, _, columns, _, width, _ = right.shape
    zb = pl.program_id(0)
    slot = lax.broadcasted_iota(jnp.int32, right.shape[4:], 0)
    for yb in range(columns):
        for a in range(rows):
            active = slot < used[a, zb * columns + yb]
            for s in range(2):
                value = right[a, 0, yb, s]
                out[yb, 0, s, a] = jnp.where(active, value, jnp.zeros_like(value))


def masked_right(far_right, used):
    rows, _, _, width, cells = far_right.shape
    right = far_right.reshape(rows, SIDE, SIDE, 2, width, cells)
    return call(
        mask_kernel,
        "mask",
        (SIDE,),
        [
            pl.BlockSpec(memory_space=pltpu.SMEM),
            pl.BlockSpec((rows, 1, SIDE, 2, width, cells), lambda z: (0, z, 0, 0, 0, 0)),
        ],
        pl.BlockSpec((SIDE, 1, 2, rows, width, cells), lambda z: (0, z, 0, 0, 0, 0)),
        jax.ShapeDtypeStruct((SIDE, SIDE, 2, rows, width, cells), far_right.dtype),
        (used, right),
        0,
    )


def turn_kernel(left, out):
    cols, planes, _, sides, width, cells = left.shape
    row = lax.broadcasted_iota(jnp.int32, (cells, cells), 0)
    column = lax.broadcasted_iota(jnp.int32, (cells, cells), 1)
    unit = jnp.where(row == column, 1.0, 0.0).astype(left.dtype)
    for c in range(sides):
        block = jnp.concatenate([left[i, j, 0, c] for i in range(cols) for j in range(planes)], axis=0)
        turned = lax.dot_general(unit, block, NT, preferred_element_type=jnp.float32)
        out[c * cells : (c + 1) * cells] = turned.astype(out.dtype)


def turned_left(far_left):
    count, sides, width, cells = far_left.shape
    cols = count // SIDE**2
    left = far_left.reshape(cols, SIDE, SIDE, sides, width, cells)
    pair = cells // (SIDE * width)
    return call(
        turn_kernel,
        "turn",
        (SIDE, cols // pair),
        [pl.BlockSpec((pair, SIDE, 1, sides, width, cells), lambda y, j: (j, 0, y, 0, 0, 0))],
        pl.BlockSpec((sides * cells, cells), lambda y, j: (0, y * (cols // pair) + j)),
        jax.ShapeDtypeStruct((sides * cells, count * width), far_left.dtype),
        (left,),
        0,
    )


def coefficient_kernel(planes, *refs):
    slips, weights, out = refs[: len(OFFSETS)], refs[len(OFFSETS)], refs[-1]
    _, _, _, rows, width, cells = weights.shape
    for i, slip in enumerate(slips):
        z = planes[i]
        parts = [weights[0, z, s].reshape(rows * width, cells) for s in range(2)]
        value = jnp.dot(
            jnp.concatenate(parts, axis=1), slip[...], preferred_element_type=jnp.float32
        )
        out[:, z] = value.astype(jnp.bfloat16).reshape(rows, width, value.shape[1])


def coefficients_of(around, planes, weights, after=()):
    depth, members = around[0].shape
    lines, count, _, rows, width, cells = weights.shape
    return call(
        coefficient_kernel,
        "coefficients",
        (lines,),
        [pl.BlockSpec(memory_space=pltpu.SMEM)]
        + [whole(v) for v in around]
        + [pl.BlockSpec((1, count, 2, rows, width, cells), lambda y: (y, 0, 0, 0, 0, 0))]
        + [ANY] * len(after),
        pl.BlockSpec((rows, count, width, members), lambda y: (y, 0, 0, 0)),
        jax.ShapeDtypeStruct((lines * rows, count, width, members), jnp.bfloat16),
        (planes, *around, weights, *after),
        2 * lines * count * rows * width * depth * members,
    )


def add_far(coef, weights, near, total):
    part = jnp.dot(weights[...], coef[...], preferred_element_type=jnp.float32)
    step = pl.program_id(0)

    @pl.when(step == 0)
    def _():
        total[...] = near[...] + part

    @pl.when(step > 0)
    def _():
        total[...] += part

    return step == pl.num_programs(0) - 1


def first_kernel(
    coef, weights, near, tractions, middle_state, half_state, columns, *refs,
):
    slips, half_tractions, new_state, total = refs[-4:]
    sides, cells, _ = tractions.shape

    @pl.when(add_far(coef, weights, near, total))
    def _():
        middle = []
        for c in range(sides):
            rates = total[c * cells : (c + 1) * cells]
            old = tractions[c]
            middle.append(old + time_step * rates)
            half_tractions[c] = old + 0.5 * time_step * rates
        state = middle_state[...]
        slip_rates, speed = friction_slip(
            middle, state, *[columns[:, k : k + 1] for k in range(3)]
        )
        for s in range(2):
            slips[s * cells : (s + 1) * cells] = slip_rates[s]
        state_rates = (jnp.exp(-state) - speed) * columns[:, 3:]
        new_state[...] = half_state[...] + 0.5 * time_step * state_rates


def second_kernel(coef, weights, near, half_tractions, *refs):
    new_tractions, total = refs[-2:]
    sides, cells, _ = half_tractions.shape

    @pl.when(add_far(coef, weights, near, total))
    def _():
        for c in range(sides):
            rates = total[c * cells : (c + 1) * cells]
            new_tractions[c] = (half_tractions[c] + 0.5 * time_step * rates).T


def far_specs(coef, weights, steps):
    depth, members = coef.shape
    return [
        pl.BlockSpec((depth // steps, members), lambda k: (k, 0)),
        pl.BlockSpec((weights.shape[0], depth // steps), lambda k: (0, k)),
    ]


def near_kernel(x0, x1, x2, weights, out):
    cells = weights.shape[3]
    total = None
    for k, x in enumerate((x0, x1, x2)):
        part = jnp.dot(
            jnp.concatenate([weights[k, 0, s] for s in range(2)], axis=1),
            x[...],
            preferred_element_type=jnp.float32,
        )
        total = part if total is None else total + part
    out[...] = total


def near_part(slabs, near_blocks):
    depth, members = slabs[0].shape
    sides, cells = near_blocks.shape[1], near_blocks.shape[3]
    return call(
        near_kernel,
        "near",
        (sides,),
        [whole(slabs[0])] * 3 + [pl.BlockSpec((3, 1, 2, cells, cells), lambda c: (0, c, 0, 0, 0))],
        pl.BlockSpec((cells, members), lambda c: (c, 0)),
        jax.ShapeDtypeStruct((sides * cells, members), jnp.float32),
        (*slabs, near_blocks),
        2 * 3 * sides * cells * depth * members,
    )


def on_device(
    tractions, log_state, rate_coef, state_coef, normal_stress, inv_length,
    near_blocks, far_right, far_left, ranks,
):
    place = {axis: lax.axis_index(axis) for axis in ALL}
    row = place["z"] * SIDE + place["y"]
    col = place["x"] * CORES + place["core"]
    tile_rows, tile_cols, _, width, cells = far_right.shape
    all_members = log_state.shape[0]
    members = all_members // PARTS
    sides = far_left.shape[2]

    block_row = row * tile_rows + jnp.arange(tile_rows, dtype=jnp.int32)
    block_col = jnp.arange(tile_cols, dtype=jnp.int32) * tile_rows + col
    near = jnp.abs(block_row[:, None] - block_col[None, :]) < 2
    right = masked_right(far_right, jnp.where(near, 0, ranks))
    right = lax.all_to_all(right, "y", split_axis=0, concat_axis=0, tiled=True)
    left = turned_left(far_left[0])
    columns = jnp.stack([rate_coef, state_coef, normal_stress, inv_length], axis=1)

    planes = jnp.stack([(place["z"] + dz) % SIDE for dz in OFFSETS])

    def gathered(slips):
        return [slips] + [from_z(slips, dz) for dz in OFFSETS[1:]]

    def sent(coef):
        coef = coef.reshape(coef.shape[0], -1, members)
        coef = lax.all_to_all(coef, ("y", "x", "core"), split_axis=0, concat_axis=0, tiled=True)
        return coef.reshape(-1, members)

    steps = 4
    flops = 2 * sides * cells * left.shape[1] * members
    scratch = [pltpu.VMEM((sides * cells, members), jnp.float32)]

    def start(part):
        here = slice(part * members, (part + 1) * members)
        old = jnp.swapaxes(tractions[:, here], 1, 2)
        state = jnp.swapaxes(log_state[here], 0, 1)
        slip_rates, speed = friction_slip(old, state, *[columns[:, k : k + 1] for k in range(3)])
        slips = jnp.concatenate(slip_rates, axis=0)
        state_rates = (jnp.exp(-state) - speed) * columns[:, 3:]
        middle_state = state + time_step * state_rates
        half_state = state + 0.5 * time_step * state_rates
        return slips, (old, middle_state, half_state, columns)

    def first_section(coef, rates_near, rest, after):
        rest = (rates_near, *rest)
        out_shape = (
            jax.ShapeDtypeStruct((2 * cells, members), jnp.bfloat16),
            jax.ShapeDtypeStruct((sides, cells, members), jnp.float32),
            jax.ShapeDtypeStruct((cells, members), jnp.float32),
        )
        return call(
            first_kernel, "first_section", (steps,),
            far_specs(coef, left, steps) + [whole(v) for v in rest] + [ANY] * len(after),
            [whole(v) for v in out_shape],
            out_shape, (coef, left, *rest, *after), flops, scratch,
        )

    def second_section(part, coef, rates_near, half_tractions, before, after):
        rest = (rates_near, half_tractions)
        return call(
            second_kernel, "second_section", (steps,),
            far_specs(coef, left, steps) + [whole(v) for v in rest]
            + [ANY] * (len(before) + len(after)),
            pl.BlockSpec((sides, members, cells), lambda k: (0, part, 0)),
            jax.ShapeDtypeStruct((sides, all_members, cells), jnp.float32),
            (coef, left, *rest, *before, *after), flops, scratch,
            {4: 0} if before else None,
        )

    def neighbours(slips):
        return [beside(slips, -1), slips, beside(slips, 1)]

    begun = [start(part) for part in range(PARTS)]
    around = [gathered(slips) for slips, _ in begun]
    near_rates = [near_part(neighbours(slips), near_blocks[0]) for slips, _ in begun]
    before = (left, columns, *near_rates, *around[1])
    coefs = [coefficients_of(around[0], planes, right, before)]
    arrived = [sent(coefs[0])]
    coefs.append(coefficients_of(around[1], planes, right, (coefs[0],)))
    arrived.append(sent(coefs[1]))
    first, beside_all = [], []
    for part in range(PARTS):
        first.append(first_section(arrived[part], near_rates[part], begun[part][1], (coefs[-1],)))
        beside_all.append(neighbours(first[part][0]))
        coefs.append(coefficients_of(gathered(first[part][0]), planes, right, beside_all[part]))
        arrived.append(sent(coefs[-1]))
    near_rates = [near_part(beside_all[part], near_blocks[0]) for part in range(PARTS)]
    after = (coefs[3], near_rates[1])
    result = second_section(0, arrived[2], near_rates[0], first[0][1], (), after)
    result = second_section(1, arrived[3], near_rates[1], first[1][1], (result,), ())
    new_state = jnp.concatenate([jnp.swapaxes(v[2], 0, 1) for v in first], axis=0)
    return (result, new_state)


def solution(mesh):
    mesh = Mesh(mesh.devices.reshape(SIDE, SIDE, SIDE, CORES), ALL)
    row, col = ("z", "y"), ("x", "core")
    placed = (
        P(None, None, ALL),
        P(None, ALL),
        P(ALL),
        P(ALL),
        P(ALL),
        P(ALL),
        P(ALL, None, None, None, None, None),
        P(row, col, None, None, None),
        P(ALL, None, None, None, None),
        P(row, col),
    )
    return jax.shard_map(
        on_device,
        mesh=mesh,
        in_specs=placed,
        out_specs=(P(None, None, ALL), P(None, ALL)),
        check_vma=False,
    )
```

```python
import functools
import math

import jax
import jax.numpy as jnp
from jax import lax
from jax.experimental import pallas as pl
from jax.experimental.pallas import tpu as pltpu
from jax.sharding import Mesh
from jax.sharding import PartitionSpec as P

time_step = 0.03
PARTS = 2
SIDE = 4
CORES = 2
OFFSETS = (0, 1, 3, 2)
ALL = ("z", "y", "x", "core")
VMEM = 65_000_000
ANY = pl.BlockSpec(memory_space=pl.ANY)
NT = (((1,), (1,)), ((), ()))


def sinh(x):
    small = x * x
    series = x * (1.0 + small * (1.0 / 6 + small * (1.0 / 120 + small * (1.0 / 5040))))
    exact = jnp.exp(x - math.log(2.0)) - jnp.exp(-x - math.log(2.0))
    return jnp.where(x < 0.35, series, exact)


def friction_slip(traction, log_value, rate_coef, state_coef, normal_stress):
    effective = jnp.maximum(normal_stress - traction[2], 1.0)
    scaled = rate_coef * effective
    shear_size = jnp.sqrt(traction[0] * traction[0] + traction[1] * traction[1])
    stress_ratio = shear_size / scaled
    amplitude = 2.0 * jnp.exp(-state_coef * log_value / rate_coef) * sinh(stress_ratio)
    factor = amplitude / (scaled * jnp.maximum(stress_ratio, 1.0))
    slip_rates = [(factor * traction[s]).astype(jnp.bfloat16) for s in range(2)]
    slip_speed = amplitude * jnp.minimum(stress_ratio, 1.0)
    return (slip_rates, slip_speed)


def beside(slabs, step):
    count = SIDE**3 * CORES
    pairs = [(i, i - step) for i in range(count) if 0 <= i - step < count]
    return lax.ppermute(slabs, ALL, pairs)


def from_z(slabs, dz):
    return lax.ppermute(slabs, "z", [((i + dz) % SIDE, i) for i in range(SIDE)])


def whole(v):
    return pl.BlockSpec(v.shape, lambda *_: (0,) * len(v.shape))


def call(kernel, name, grid, in_specs, out_specs, out_shape, args, flops, scratch=(), aliases=None):
    return pl.pallas_call(
        kernel,
        grid=grid,
        in_specs=in_specs,
        out_specs=out_specs,
        out_shape=out_shape,
        scratch_shapes=list(scratch),
        input_output_aliases=aliases or {},
        compiler_params=pltpu.CompilerParams(vmem_limit_bytes=VMEM),
        cost_estimate=pl.CostEstimate(flops=flops, bytes_accessed=8 * 2**20, transcendentals=0),
        name=name,
    )(*args)


def mask_kernel(place, ranks, right, out):
    rows, _, lines, _, width, _ = right.shape
    zb = pl.program_id(0)
    first_row, col = place[0] * rows, place[1]
    slot = lax.broadcasted_iota(jnp.int32, right.shape[4:], 0)
    for yb in range(lines):
        b = zb * lines + yb
        for a in range(rows):
            near = jnp.abs(first_row + a - (b * rows + col)) < 2
            used = jnp.where(near, 0, ranks[a, b])
            for s in range(2):
                value = right[a, 0, yb, s]
                out[yb, 0, s, a] = jnp.where(slot < used, value, jnp.zeros_like(value))


def masked_right(far_right, ranks, place):
    rows, _, _, width, cells = far_right.shape
    right = far_right.reshape(rows, SIDE, SIDE, 2, width, cells)
    scalars = pl.BlockSpec(memory_space=pltpu.SMEM)
    return call(
        mask_kernel,
        "mask",
        (SIDE,),
        [
            scalars,
            scalars,
            pl.BlockSpec((rows, 1, SIDE, 2, width, cells), lambda z: (0, z, 0, 0, 0, 0)),
        ],
        pl.BlockSpec((SIDE, 1, 2, rows, width, cells), lambda z: (0, z, 0, 0, 0, 0)),
        jax.ShapeDtypeStruct((SIDE, SIDE, 2, rows, width, cells), far_right.dtype),
        (place, ranks, right),
        0,
    )


def turn_kernel(left, out):
    cols, planes, _, sides, width, cells = left.shape
    row = lax.broadcasted_iota(jnp.int32, (cells, cells), 0)
    column = lax.broadcasted_iota(jnp.int32, (cells, cells), 1)
    unit = jnp.where(row == column, 1.0, 0.0).astype(left.dtype)
    for c in range(sides):
        block = jnp.concatenate([left[i, j, 0, c] for i in range(cols) for j in range(planes)], axis=0)
        turned = lax.dot_general(unit, block, NT, preferred_element_type=jnp.float32)
        out[c * cells : (c + 1) * cells] = turned.astype(out.dtype)


def turned_left(far_left):
    count, sides, width, cells = far_left.shape
    cols = count // SIDE**2
    left = far_left.reshape(cols, SIDE, SIDE, sides, width, cells)
    pair = cells // (SIDE * width)
    return call(
        turn_kernel,
        "turn",
        (SIDE, cols // pair),
        [pl.BlockSpec((pair, SIDE, 1, sides, width, cells), lambda y, j: (j, 0, y, 0, 0, 0))],
        pl.BlockSpec((sides * cells, cells), lambda y, j: (0, y * (cols // pair) + j)),
        jax.ShapeDtypeStruct((sides * cells, count * width), far_left.dtype),
        (left,),
        0,
    )


def coefficient_kernel(planes, *refs):
    slips, weights, out = refs[: len(OFFSETS)], refs[len(OFFSETS)], refs[-1]
    _, _, _, rows, width, cells = weights.shape
    for i, slip in enumerate(slips):
        z = planes[i]
        parts = [weights[0, z, s].reshape(rows * width, cells) for s in range(2)]
        value = jnp.dot(
            jnp.concatenate(parts, axis=1), slip[...], preferred_element_type=jnp.float32
        )
        out[:, z] = value.astype(jnp.bfloat16).reshape(rows, width, value.shape[1])


def coefficients_of(around, planes, weights, after=()):
    depth, members = around[0].shape
    lines, count, _, rows, width, cells = weights.shape
    return call(
        coefficient_kernel,
        "coefficients",
        (lines,),
        [pl.BlockSpec(memory_space=pltpu.SMEM)]
        + [whole(v) for v in around]
        + [pl.BlockSpec((1, count, 2, rows, width, cells), lambda y: (y, 0, 0, 0, 0, 0))]
        + [ANY] * len(after),
        pl.BlockSpec((rows, count, width, members), lambda y: (y, 0, 0, 0)),
        jax.ShapeDtypeStruct((lines * rows, count, width, members), jnp.bfloat16),
        (planes, *around, weights, *after),
        2 * lines * count * rows * width * depth * members,
    )


def add_far(coef, weights, near, total):
    part = jnp.dot(weights[...], coef[...], preferred_element_type=jnp.float32)
    step = pl.program_id(0)

    @pl.when(step == 0)
    def _():
        total[...] = near[...] + part

    @pl.when(step > 0)
    def _():
        total[...] += part

    return step == pl.num_programs(0) - 1


def first_kernel(
    coef, weights, near, tractions, middle_state, half_state, columns, *refs,
):
    slips, half_tractions, new_state, total = refs[-4:]
    sides, cells, _ = tractions.shape

    @pl.when(add_far(coef, weights, near, total))
    def _():
        middle = []
        for c in range(sides):
            rates = total[c * cells : (c + 1) * cells]
            old = tractions[c]
            middle.append(old + time_step * rates)
            half_tractions[c] = old + 0.5 * time_step * rates
        state = middle_state[...]
        slip_rates, speed = friction_slip(
            middle, state, *[columns[:, k : k + 1] for k in range(3)]
        )
        for s in range(2):
            slips[s * cells : (s + 1) * cells] = slip_rates[s]
        state_rates = (jnp.exp(-state) - speed) * columns[:, 3:]
        new_state[...] = half_state[...] + 0.5 * time_step * state_rates


def second_kernel(coef, weights, x0, x1, x2, near_blocks, half_tractions, *refs):
    new_tractions, total = refs[-2:]
    sides, cells, _ = half_tractions.shape
    part = jnp.dot(weights[...], coef[...], preferred_element_type=jnp.float32)
    step = pl.program_id(0)

    @pl.when(step == 0)
    def _():
        for c in range(sides):
            here = slice(c * cells, (c + 1) * cells)
            total[here] = near_product((x0, x1, x2), near_blocks, c) + part[here]

    @pl.when(step > 0)
    def _():
        total[...] += part

    @pl.when(step == pl.num_programs(0) - 1)
    def _():
        for c in range(sides):
            rates = total[c * cells : (c + 1) * cells]
            new_tractions[c] = (half_tractions[c] + 0.5 * time_step * rates).T


def far_specs(coef, weights, steps):
    depth, members = coef.shape
    return [
        pl.BlockSpec((depth // steps, members), lambda k: (k, 0)),
        pl.BlockSpec((weights.shape[0], depth // steps), lambda k: (0, k)),
    ]


def near_product(slabs, weights, c):
    total = None
    for k, x in enumerate(slabs):
        part = jnp.dot(
            jnp.concatenate([weights[k, c, s] for s in range(2)], axis=1),
            x[...],
            preferred_element_type=jnp.float32,
        )
        total = part if total is None else total + part
    return total


def near_kernel(x0, x1, x2, weights, out):
    out[...] = near_product((x0, x1, x2), weights, 0)


def near_part(slabs, near_blocks):
    depth, members = slabs[0].shape
    sides, cells = near_blocks.shape[1], near_blocks.shape[3]
    return call(
        near_kernel,
        "near",
        (sides,),
        [whole(slabs[0])] * 3 + [pl.BlockSpec((3, 1, 2, cells, cells), lambda c: (0, c, 0, 0, 0))],
        pl.BlockSpec((cells, members), lambda c: (c, 0)),
        jax.ShapeDtypeStruct((sides * cells, members), jnp.float32),
        (*slabs, near_blocks),
        2 * 3 * sides * cells * depth * members,
    )


def on_device(
    tractions, log_state, rate_coef, state_coef, normal_stress, inv_length,
    near_blocks, far_right, far_left, ranks,
):
    place = {axis: lax.axis_index(axis) for axis in ALL}
    row = place["z"] * SIDE + place["y"]
    col = place["x"] * CORES + place["core"]
    cells = far_right.shape[-1]
    all_members = log_state.shape[0]
    members = all_members // PARTS
    sides = far_left.shape[2]

    right = masked_right(far_right, ranks, jnp.stack([row, col]))
    right = lax.all_to_all(right, "y", split_axis=0, concat_axis=0, tiled=True)
    left = turned_left(far_left[0])
    columns = jnp.stack([rate_coef, state_coef, normal_stress, inv_length], axis=1)

    planes = jnp.stack([(place["z"] + dz) % SIDE for dz in OFFSETS])

    def gathered(slips):
        return [slips] + [from_z(slips, dz) for dz in OFFSETS[1:]]

    def sent(coef):
        coef = coef.reshape(coef.shape[0], -1, members)
        coef = lax.all_to_all(coef, ("y", "x", "core"), split_axis=0, concat_axis=0, tiled=True)
        return coef.reshape(-1, members)

    steps = 4
    flops = 2 * sides * cells * left.shape[1] * members
    scratch = [pltpu.VMEM((sides * cells, members), jnp.float32)]

    def start(part):
        here = slice(part * members, (part + 1) * members)
        old = jnp.swapaxes(tractions[:, here], 1, 2)
        state = jnp.swapaxes(log_state[here], 0, 1)
        slip_rates, speed = friction_slip(old, state, *[columns[:, k : k + 1] for k in range(3)])
        slips = jnp.concatenate(slip_rates, axis=0)
        state_rates = (jnp.exp(-state) - speed) * columns[:, 3:]
        middle_state = state + time_step * state_rates
        half_state = state + 0.5 * time_step * state_rates
        return slips, (old, middle_state, half_state, columns)

    def first_section(coef, rates_near, rest, after):
        rest = (rates_near, *rest)
        out_shape = (
            jax.ShapeDtypeStruct((2 * cells, members), jnp.bfloat16),
            jax.ShapeDtypeStruct((sides, cells, members), jnp.float32),
            jax.ShapeDtypeStruct((cells, members), jnp.float32),
        )
        return call(
            first_kernel, "first_section", (steps,),
            far_specs(coef, left, steps) + [whole(v) for v in rest] + [ANY] * len(after),
            [whole(v) for v in out_shape],
            out_shape, (coef, left, *rest, *after), flops, scratch,
        )

    def second_section(part, coef, slabs, half_tractions, before, after):
        rest = (*slabs, near_blocks[0], half_tractions)
        return call(
            second_kernel, "second_section", (steps,),
            far_specs(coef, left, steps) + [whole(v) for v in rest]
            + [ANY] * (len(before) + len(after)),
            pl.BlockSpec((sides, members, cells), lambda k: (0, part, 0)),
            jax.ShapeDtypeStruct((sides, all_members, cells), jnp.float32),
            (coef, left, *rest, *before, *after), flops, scratch,
            {7: 0} if before else None,
        )

    def neighbours(slips):
        return [beside(slips, -1), slips, beside(slips, 1)]

    begun = [start(part) for part in range(PARTS)]
    around = [gathered(slips) for slips, _ in begun]
    near_rates = [near_part(neighbours(slips), near_blocks[0]) for slips, _ in begun]
    before = (left, columns, *near_rates, *around[1])
    coefs = [coefficients_of(around[0], planes, right, before)]
    arrived = [sent(coefs[0])]
    coefs.append(coefficients_of(around[1], planes, right, (coefs[0],)))
    arrived.append(sent(coefs[1]))
    first, slabs = [], []
    for part in range(PARTS):
        first.append(first_section(arrived[part], near_rates[part], begun[part][1], (coefs[-1],)))
        slabs.append(neighbours(first[part][0]))
        early = slabs[0] if part == 0 else ()
        coefs.append(coefficients_of(gathered(first[part][0]), planes, right, early))
        arrived.append(sent(coefs[-1]))
    result = second_section(0, arrived[2], slabs[0], first[0][1], (), (coefs[3],))
    result = second_section(1, arrived[3], slabs[1], first[1][1], (result,), ())
    new_state = jnp.concatenate([jnp.swapaxes(v[2], 0, 1) for v in first], axis=0)
    return (result, new_state)


def solution(mesh):
    mesh = Mesh(mesh.devices.reshape(SIDE, SIDE, SIDE, CORES), ALL)
    row, col = ("z", "y"), ("x", "core")
    placed = (
        P(None, None, ALL),
        P(None, ALL),
        P(ALL),
        P(ALL),
        P(ALL),
        P(ALL),
        P(ALL, None, None, None, None, None),
        P(row, col, None, None, None),
        P(ALL, None, None, None, None),
        P(row, col),
    )
    return jax.shard_map(
        on_device,
        mesh=mesh,
        in_specs=placed,
        out_specs=(P(None, None, ALL), P(None, ALL)),
        check_vma=False,
    )
```

```python
import functools
import math

import jax
import jax.numpy as jnp
from jax import lax
from jax.experimental import pallas as pl
from jax.experimental.pallas import tpu as pltpu
from jax.sharding import Mesh
from jax.sharding import PartitionSpec as P

time_step = 0.03
PARTS = 2
SIDE = 4
CORES = 2
OFFSETS = (0, 1, 3, 2)
ALL = ("z", "y", "x", "core")
VMEM = 65_000_000
ANY = pl.BlockSpec(memory_space=pl.ANY)
NT = (((1,), (1,)), ((), ()))


def sinh(x):
    small = x * x
    series = x * (1.0 + small * (1.0 / 6 + small * (1.0 / 120 + small * (1.0 / 5040))))
    exact = jnp.exp(x - math.log(2.0)) - jnp.exp(-x - math.log(2.0))
    return jnp.where(x < 0.35, series, exact)


def friction_slip(traction, log_value, rate_coef, state_coef, normal_stress):
    effective = jnp.maximum(normal_stress - traction[2], 1.0)
    scaled = rate_coef * effective
    shear_size = jnp.sqrt(traction[0] * traction[0] + traction[1] * traction[1])
    stress_ratio = shear_size / scaled
    amplitude = 2.0 * jnp.exp(-state_coef * log_value / rate_coef) * sinh(stress_ratio)
    factor = amplitude / (scaled * jnp.maximum(stress_ratio, 1.0))
    slip_rates = [(factor * traction[s]).astype(jnp.bfloat16) for s in range(2)]
    slip_speed = amplitude * jnp.minimum(stress_ratio, 1.0)
    return (slip_rates, slip_speed)


def beside(slabs, step):
    count = SIDE**3 * CORES
    pairs = [(i, i - step) for i in range(count) if 0 <= i - step < count]
    return lax.ppermute(slabs, ALL, pairs)


def from_z(slabs, dz):
    return lax.ppermute(slabs, "z", [((i + dz) % SIDE, i) for i in range(SIDE)])


def whole(v):
    return pl.BlockSpec(v.shape, lambda *_: (0,) * len(v.shape))


def call(kernel, name, grid, in_specs, out_specs, out_shape, args, flops, scratch=(), aliases=None):
    return pl.pallas_call(
        kernel,
        grid=grid,
        in_specs=in_specs,
        out_specs=out_specs,
        out_shape=out_shape,
        scratch_shapes=list(scratch),
        input_output_aliases=aliases or {},
        compiler_params=pltpu.CompilerParams(vmem_limit_bytes=VMEM),
        cost_estimate=pl.CostEstimate(flops=flops, bytes_accessed=8 * 2**20, transcendentals=0),
        name=name,
    )(*args)


def mask_kernel(place, ranks, right, out):
    rows, _, lines, _, width, _ = right.shape
    zb = pl.program_id(0)
    first_row, col = place[0] * rows, place[1]
    slot = lax.broadcasted_iota(jnp.int32, right.shape[4:], 0)
    for yb in range(lines):
        b = zb * lines + yb
        for a in range(rows):
            near = jnp.abs(first_row + a - (b * rows + col)) < 2
            used = jnp.where(near, 0, ranks[a, b])
            for s in range(2):
                value = right[a, 0, yb, s]
                out[yb, 0, s, a] = jnp.where(slot < used, value, jnp.zeros_like(value))


def masked_right(far_right, ranks, place):
    rows, _, _, width, cells = far_right.shape
    right = far_right.reshape(rows, SIDE, SIDE, 2, width, cells)
    scalars = pl.BlockSpec(memory_space=pltpu.SMEM)
    return call(
        mask_kernel,
        "mask",
        (SIDE,),
        [
            scalars,
            scalars,
            pl.BlockSpec((rows, 1, SIDE, 2, width, cells), lambda z: (0, z, 0, 0, 0, 0)),
        ],
        pl.BlockSpec((SIDE, 1, 2, rows, width, cells), lambda z: (0, z, 0, 0, 0, 0)),
        jax.ShapeDtypeStruct((SIDE, SIDE, 2, rows, width, cells), far_right.dtype),
        (place, ranks, right),
        0,
    )


def turn_kernel(left, out):
    cols, planes, _, sides, width, cells = left.shape
    row = lax.broadcasted_iota(jnp.int32, (cells, cells), 0)
    column = lax.broadcasted_iota(jnp.int32, (cells, cells), 1)
    unit = jnp.where(row == column, 1.0, 0.0).astype(left.dtype)
    for c in range(sides):
        block = jnp.concatenate([left[i, j, 0, c] for i in range(cols) for j in range(planes)], axis=0)
        turned = lax.dot_general(unit, block, NT, preferred_element_type=jnp.float32)
        out[c * cells : (c + 1) * cells] = turned.astype(out.dtype)


def turned_left(far_left):
    count, sides, width, cells = far_left.shape
    cols = count // SIDE**2
    left = far_left.reshape(cols, SIDE, SIDE, sides, width, cells)
    pair = cells // (SIDE * width)
    return call(
        turn_kernel,
        "turn",
        (SIDE, cols // pair),
        [pl.BlockSpec((pair, SIDE, 1, sides, width, cells), lambda y, j: (j, 0, y, 0, 0, 0))],
        pl.BlockSpec((sides * cells, cells), lambda y, j: (0, y * (cols // pair) + j)),
        jax.ShapeDtypeStruct((sides * cells, count * width), far_left.dtype),
        (left,),
        0,
    )


def coefficient_kernel(planes, *refs):
    slips, weights, out = refs[: len(OFFSETS)], refs[len(OFFSETS)], refs[-1]
    _, _, _, rows, width, cells = weights.shape
    for i, slip in enumerate(slips):
        z = planes[i]
        parts = [weights[0, z, s].reshape(rows * width, cells) for s in range(2)]
        value = jnp.dot(
            jnp.concatenate(parts, axis=1), slip[...], preferred_element_type=jnp.float32
        )
        out[:, z] = value.astype(jnp.bfloat16).reshape(rows, width, value.shape[1])


def coefficients_of(around, planes, weights, after=()):
    depth, members = around[0].shape
    lines, count, _, rows, width, cells = weights.shape
    return call(
        coefficient_kernel,
        "coefficients",
        (lines,),
        [pl.BlockSpec(memory_space=pltpu.SMEM)]
        + [whole(v) for v in around]
        + [pl.BlockSpec((1, count, 2, rows, width, cells), lambda y: (y, 0, 0, 0, 0, 0))]
        + [ANY] * len(after),
        pl.BlockSpec((rows, count, width, members), lambda y: (y, 0, 0, 0)),
        jax.ShapeDtypeStruct((lines * rows, count, width, members), jnp.bfloat16),
        (planes, *around, weights, *after),
        2 * lines * count * rows * width * depth * members,
    )


def add_far(coef, weights, near, total):
    part = jnp.dot(weights[...], coef[...], preferred_element_type=jnp.float32)
    step = pl.program_id(0)

    @pl.when(step == 0)
    def _():
        total[...] = near[...] + part

    @pl.when(step > 0)
    def _():
        total[...] += part

    return step == pl.num_programs(0) - 1


def first_kernel(
    coef, weights, near, tractions, middle_state, half_state, columns, *refs,
):
    slips, half_tractions, new_state, total = refs[-4:]
    sides, cells, _ = tractions.shape

    @pl.when(add_far(coef, weights, near, total))
    def _():
        middle = []
        for c in range(sides):
            rates = total[c * cells : (c + 1) * cells]
            old = tractions[c]
            middle.append(old + time_step * rates)
            half_tractions[c] = old + 0.5 * time_step * rates
        state = middle_state[...]
        slip_rates, speed = friction_slip(
            middle, state, *[columns[:, k : k + 1] for k in range(3)]
        )
        for s in range(2):
            slips[s * cells : (s + 1) * cells] = slip_rates[s]
        state_rates = (jnp.exp(-state) - speed) * columns[:, 3:]
        new_state[...] = half_state[...] + 0.5 * time_step * state_rates


def second_kernel(coef, weights, x0, x1, x2, near_blocks, half_tractions, *refs):
    new_tractions, total = refs[-2:]
    sides, cells, _ = half_tractions.shape
    part = jnp.dot(weights[...], coef[...], preferred_element_type=jnp.float32)
    step = pl.program_id(0)

    @pl.when(step == 0)
    def _():
        for c in range(sides):
            here = slice(c * cells, (c + 1) * cells)
            total[here] = near_product((x0, x1, x2), near_blocks, c) + part[here]

    @pl.when(step > 0)
    def _():
        total[...] += part

    @pl.when(step == pl.num_programs(0) - 1)
    def _():
        for c in range(sides):
            rates = total[c * cells : (c + 1) * cells]
            new_tractions[c] = (half_tractions[c] + 0.5 * time_step * rates).T


def far_specs(coef, weights, steps):
    depth, members = coef.shape
    return [
        pl.BlockSpec((depth // steps, members), lambda k: (k, 0)),
        pl.BlockSpec((weights.shape[0], depth // steps), lambda k: (0, k)),
    ]


def near_product(slabs, weights, c):
    total = None
    for k, x in enumerate(slabs):
        part = jnp.dot(
            jnp.concatenate([weights[k, c, s] for s in range(2)], axis=1),
            x[...],
            preferred_element_type=jnp.float32,
        )
        total = part if total is None else total + part
    return total


def near_kernel(x0, x1, x2, weights, *refs):
    out = refs[-1]
    out[...] = near_product((x0, x1, x2), weights, 0)


def near_part(slabs, near_blocks, after):
    depth, members = slabs[0].shape
    sides, cells = near_blocks.shape[1], near_blocks.shape[3]
    return call(
        near_kernel,
        "near",
        (sides,),
        [whole(slabs[0])] * 3 + [pl.BlockSpec((3, 1, 2, cells, cells), lambda c: (0, c, 0, 0, 0))]
        + [ANY] * len(after),
        pl.BlockSpec((cells, members), lambda c: (c, 0)),
        jax.ShapeDtypeStruct((sides * cells, members), jnp.float32),
        (*slabs, near_blocks, *after),
        2 * 3 * sides * cells * depth * members,
    )


def on_device(
    tractions, log_state, rate_coef, state_coef, normal_stress, inv_length,
    near_blocks, far_right, far_left, ranks,
):
    place = {axis: lax.axis_index(axis) for axis in ALL}
    row = place["z"] * SIDE + place["y"]
    col = place["x"] * CORES + place["core"]
    cells = far_right.shape[-1]
    all_members = log_state.shape[0]
    members = all_members // PARTS
    sides = far_left.shape[2]

    right = masked_right(far_right, ranks, jnp.stack([row, col]))
    right = lax.all_to_all(right, "y", split_axis=0, concat_axis=0, tiled=True)
    left = turned_left(far_left[0])
    columns = jnp.stack([rate_coef, state_coef, normal_stress, inv_length], axis=1)

    planes = jnp.stack([(place["z"] + dz) % SIDE for dz in OFFSETS])

    def gathered(slips):
        return [slips] + [from_z(slips, dz) for dz in OFFSETS[1:]]

    def sent(coef):
        coef = coef.reshape(coef.shape[0], -1, members)
        coef = lax.all_to_all(coef, ("y", "x", "core"), split_axis=0, concat_axis=0, tiled=True)
        return coef.reshape(-1, members)

    steps = 4
    flops = 2 * sides * cells * left.shape[1] * members
    scratch = [pltpu.VMEM((sides * cells, members), jnp.float32)]

    def start(part):
        here = slice(part * members, (part + 1) * members)
        old = jnp.swapaxes(tractions[:, here], 1, 2)
        state = jnp.swapaxes(log_state[here], 0, 1)
        slip_rates, speed = friction_slip(old, state, *[columns[:, k : k + 1] for k in range(3)])
        slips = jnp.concatenate(slip_rates, axis=0)
        state_rates = (jnp.exp(-state) - speed) * columns[:, 3:]
        middle_state = state + time_step * state_rates
        half_state = state + 0.5 * time_step * state_rates
        return slips, (old, middle_state, half_state, columns)

    def first_section(coef, rates_near, rest, after):
        rest = (rates_near, *rest)
        out_shape = (
            jax.ShapeDtypeStruct((2 * cells, members), jnp.bfloat16),
            jax.ShapeDtypeStruct((sides, cells, members), jnp.float32),
            jax.ShapeDtypeStruct((cells, members), jnp.float32),
        )
        return call(
            first_kernel, "first_section", (steps,),
            far_specs(coef, left, steps) + [whole(v) for v in rest] + [ANY] * len(after),
            [whole(v) for v in out_shape],
            out_shape, (coef, left, *rest, *after), flops, scratch,
        )

    def second_section(part, coef, slabs, half_tractions, before, after):
        rest = (*slabs, near_blocks[0], half_tractions)
        return call(
            second_kernel, "second_section", (steps,),
            far_specs(coef, left, steps) + [whole(v) for v in rest]
            + [ANY] * (len(before) + len(after)),
            pl.BlockSpec((sides, members, cells), lambda k: (0, part, 0)),
            jax.ShapeDtypeStruct((sides, all_members, cells), jnp.float32),
            (coef, left, *rest, *before, *after), flops, scratch,
            {7: 0} if before else None,
        )

    def neighbours(slips):
        return [beside(slips, -1), slips, beside(slips, 1)]

    begun = [start(part) for part in range(PARTS)]
    around = [gathered(slips) for slips, _ in begun]
    slabs = [neighbours(slips) for slips, _ in begun]
    before = (left, columns, *around[1])
    coefs = [coefficients_of(around[0], planes, right, before)]
    arrived = [sent(coefs[0])]
    coefs.append(coefficients_of(around[1], planes, right, (coefs[0],)))
    arrived.append(sent(coefs[1]))
    near_rates = [near_part(v, near_blocks[0], (coefs[1],)) for v in slabs]
    first, slabs = [], []
    for part in range(PARTS):
        first.append(first_section(arrived[part], near_rates[part], begun[part][1], (coefs[-1],)))
        slabs.append(neighbours(first[part][0]))
        early = slabs[0] if part == 0 else ()
        coefs.append(coefficients_of(gathered(first[part][0]), planes, right, early))
        arrived.append(sent(coefs[-1]))
    result = second_section(0, arrived[2], slabs[0], first[0][1], (), (coefs[3],))
    result = second_section(1, arrived[3], slabs[1], first[1][1], (result,), ())
    new_state = jnp.concatenate([jnp.swapaxes(v[2], 0, 1) for v in first], axis=0)
    return (result, new_state)


def solution(mesh):
    mesh = Mesh(mesh.devices.reshape(SIDE, SIDE, SIDE, CORES), ALL)
    row, col = ("z", "y"), ("x", "core")
    placed = (
        P(None, None, ALL),
        P(None, ALL),
        P(ALL),
        P(ALL),
        P(ALL),
        P(ALL),
        P(ALL, None, None, None, None, None),
        P(row, col, None, None, None),
        P(ALL, None, None, None, None),
        P(row, col),
    )
    return jax.shard_map(
        on_device,
        mesh=mesh,
        in_specs=placed,
        out_specs=(P(None, None, ALL), P(None, ALL)),
        check_vma=False,
    )
```

```python
import functools
import math

import jax
import jax.numpy as jnp
from jax import lax
from jax.experimental import pallas as pl
from jax.experimental.pallas import tpu as pltpu
from jax.sharding import Mesh
from jax.sharding import PartitionSpec as P

time_step = 0.03
PARTS = 2
SIDE = 4
CORES = 2
OFFSETS = (0, 1, 3, 2)
ALL = ("z", "y", "x", "core")
VMEM = 65_000_000
ANY = pl.BlockSpec(memory_space=pl.ANY)
NT = (((1,), (1,)), ((), ()))


def sinh(x):
    small = x * x
    series = x * (1.0 + small * (1.0 / 6 + small * (1.0 / 120 + small * (1.0 / 5040))))
    exact = jnp.exp(x - math.log(2.0)) - jnp.exp(-x - math.log(2.0))
    return jnp.where(x < 0.35, series, exact)


def friction_slip(traction, log_value, rate_coef, state_coef, normal_stress):
    effective = jnp.maximum(normal_stress - traction[2], 1.0)
    scaled = rate_coef * effective
    shear_size = jnp.sqrt(traction[0] * traction[0] + traction[1] * traction[1])
    stress_ratio = shear_size / scaled
    amplitude = 2.0 * jnp.exp(-state_coef * log_value / rate_coef) * sinh(stress_ratio)
    factor = amplitude / (scaled * jnp.maximum(stress_ratio, 1.0))
    slip_rates = [(factor * traction[s]).astype(jnp.bfloat16) for s in range(2)]
    slip_speed = amplitude * jnp.minimum(stress_ratio, 1.0)
    return (slip_rates, slip_speed)


def beside(slabs, step):
    count = SIDE**3 * CORES
    pairs = [(i, i - step) for i in range(count) if 0 <= i - step < count]
    return lax.ppermute(slabs, ALL, pairs)


def from_z(slabs, dz):
    return lax.ppermute(slabs, "z", [((i + dz) % SIDE, i) for i in range(SIDE)])


def whole(v):
    return pl.BlockSpec(v.shape, lambda *_: (0,) * len(v.shape))


def call(kernel, name, grid, in_specs, out_specs, out_shape, args, flops, scratch=(), aliases=None):
    return pl.pallas_call(
        kernel,
        grid=grid,
        in_specs=in_specs,
        out_specs=out_specs,
        out_shape=out_shape,
        scratch_shapes=list(scratch),
        input_output_aliases=aliases or {},
        compiler_params=pltpu.CompilerParams(vmem_limit_bytes=VMEM),
        cost_estimate=pl.CostEstimate(flops=flops, bytes_accessed=8 * 2**20, transcendentals=0),
        name=name,
    )(*args)


def mask_kernel(place, ranks, right, out):
    rows, _, lines, _, width, _ = right.shape
    zb = pl.program_id(0)
    first_row, col = place[0] * rows, place[1]
    slot = lax.broadcasted_iota(jnp.int32, right.shape[4:], 0)
    for yb in range(lines):
        b = zb * lines + yb
        for a in range(rows):
            near = jnp.abs(first_row + a - (b * rows + col)) < 2
            used = jnp.where(near, 0, ranks[a, b])
            for s in range(2):
                value = right[a, 0, yb, s]
                out[yb, 0, s, a] = jnp.where(slot < used, value, jnp.zeros_like(value))


def masked_right(far_right, ranks, place):
    rows, _, _, width, cells = far_right.shape
    right = far_right.reshape(rows, SIDE, SIDE, 2, width, cells)
    scalars = pl.BlockSpec(memory_space=pltpu.SMEM)
    return call(
        mask_kernel,
        "mask",
        (SIDE,),
        [
            scalars,
            scalars,
            pl.BlockSpec((rows, 1, SIDE, 2, width, cells), lambda z: (0, z, 0, 0, 0, 0)),
        ],
        pl.BlockSpec((SIDE, 1, 2, rows, width, cells), lambda z: (0, z, 0, 0, 0, 0)),
        jax.ShapeDtypeStruct((SIDE, SIDE, 2, rows, width, cells), far_right.dtype),
        (place, ranks, right),
        0,
    )


def turn_kernel(left, out):
    cols, planes, _, sides, width, cells = left.shape
    row = lax.broadcasted_iota(jnp.int32, (cells, cells), 0)
    column = lax.broadcasted_iota(jnp.int32, (cells, cells), 1)
    unit = jnp.where(row == column, 1.0, 0.0).astype(left.dtype)
    for c in range(sides):
        block = jnp.concatenate([left[i, j, 0, c] for i in range(cols) for j in range(planes)], axis=0)
        turned = lax.dot_general(unit, block, NT, preferred_element_type=jnp.float32)
        out[c * cells : (c + 1) * cells] = turned.astype(out.dtype)


def turned_left(far_left):
    count, sides, width, cells = far_left.shape
    cols = count // SIDE**2
    left = far_left.reshape(cols, SIDE, SIDE, sides, width, cells)
    pair = cells // (SIDE * width)
    return call(
        turn_kernel,
        "turn",
        (SIDE, cols // pair),
        [pl.BlockSpec((pair, SIDE, 1, sides, width, cells), lambda y, j: (j, 0, y, 0, 0, 0))],
        pl.BlockSpec((sides * cells, cells), lambda y, j: (0, y * (cols // pair) + j)),
        jax.ShapeDtypeStruct((sides * cells, count * width), far_left.dtype),
        (left,),
        0,
    )


def coefficient_kernel(planes, *refs):
    slips, weights, out = refs[: len(OFFSETS)], refs[len(OFFSETS)], refs[-1]
    _, _, _, rows, width, cells = weights.shape
    for i, slip in enumerate(slips):
        z = planes[i]
        parts = [weights[0, z, s].reshape(rows * width, cells) for s in range(2)]
        value = jnp.dot(
            jnp.concatenate(parts, axis=1), slip[...], preferred_element_type=jnp.float32
        )
        out[:, z] = value.astype(jnp.bfloat16).reshape(rows, width, value.shape[1])


def coefficients_of(around, planes, weights, after=()):
    depth, members = around[0].shape
    lines, count, _, rows, width, cells = weights.shape
    return call(
        coefficient_kernel,
        "coefficients",
        (lines,),
        [pl.BlockSpec(memory_space=pltpu.SMEM)]
        + [whole(v) for v in around]
        + [pl.BlockSpec((1, count, 2, rows, width, cells), lambda y: (y, 0, 0, 0, 0, 0))]
        + [ANY] * len(after),
        pl.BlockSpec((rows, count, width, members), lambda y: (y, 0, 0, 0)),
        jax.ShapeDtypeStruct((lines * rows, count, width, members), jnp.bfloat16),
        (planes, *around, weights, *after),
        2 * lines * count * rows * width * depth * members,
    )


def add_far(coef, weights, near, total):
    part = jnp.dot(weights[...], coef[...], preferred_element_type=jnp.float32)
    step = pl.program_id(0)

    @pl.when(step == 0)
    def _():
        total[...] = near[...] + part

    @pl.when(step > 0)
    def _():
        total[...] += part

    return step == pl.num_programs(0) - 1


def first_kernel(
    coef, weights, near, tractions, middle_state, half_state, columns, *refs,
):
    slips, half_tractions, new_state, total = refs[-4:]
    sides, cells, _ = tractions.shape

    @pl.when(add_far(coef, weights, near, total))
    def _():
        middle = []
        for c in range(sides):
            rates = total[c * cells : (c + 1) * cells]
            old = tractions[c]
            middle.append(old + time_step * rates)
            half_tractions[c] = old + 0.5 * time_step * rates
        state = middle_state[...]
        slip_rates, speed = friction_slip(
            middle, state, *[columns[:, k : k + 1] for k in range(3)]
        )
        for s in range(2):
            slips[s * cells : (s + 1) * cells] = slip_rates[s]
        state_rates = (jnp.exp(-state) - speed) * columns[:, 3:]
        new_state[...] = half_state[...] + 0.5 * time_step * state_rates


def second_kernel(coef, weights, x0, x1, x2, near_blocks, half_tractions, *refs):
    new_tractions, total = refs[-2:]
    sides, cells, _ = half_tractions.shape
    part = jnp.dot(weights[...], coef[...], preferred_element_type=jnp.float32)
    step = pl.program_id(0)

    @pl.when(step == 0)
    def _():
        for c in range(sides):
            here = slice(c * cells, (c + 1) * cells)
            total[here] = near_product((x0, x1, x2), near_blocks, c) + part[here]

    @pl.when(step > 0)
    def _():
        total[...] += part

    @pl.when(step == pl.num_programs(0) - 1)
    def _():
        for c in range(sides):
            rates = total[c * cells : (c + 1) * cells]
            new_tractions[c] = (half_tractions[c] + 0.5 * time_step * rates).T


def far_specs(coef, weights, steps):
    depth, members = coef.shape
    return [
        pl.BlockSpec((depth // steps, members), lambda k: (k, 0)),
        pl.BlockSpec((weights.shape[0], depth // steps), lambda k: (0, k)),
    ]


def near_product(slabs, weights, c):
    total = None
    for k, x in enumerate(slabs):
        part = jnp.dot(
            jnp.concatenate([weights[k, c, s] for s in range(2)], axis=1),
            x[...],
            preferred_element_type=jnp.float32,
        )
        total = part if total is None else total + part
    return total


def near_kernel(x0, x1, x2, weights, *refs):
    out = refs[-1]
    out[...] = near_product((x0, x1, x2), weights, 0)


def near_part(slabs, near_blocks, after):
    depth, members = slabs[0].shape
    sides, cells = near_blocks.shape[1], near_blocks.shape[3]
    return call(
        near_kernel,
        "near",
        (sides,),
        [whole(slabs[0])] * 3 + [pl.BlockSpec((3, 1, 2, cells, cells), lambda c: (0, c, 0, 0, 0))]
        + [ANY] * len(after),
        pl.BlockSpec((cells, members), lambda c: (c, 0)),
        jax.ShapeDtypeStruct((sides * cells, members), jnp.float32),
        (*slabs, near_blocks, *after),
        2 * 3 * sides * cells * depth * members,
    )


def on_device(
    tractions, log_state, rate_coef, state_coef, normal_stress, inv_length,
    near_blocks, far_right, far_left, ranks,
):
    place = {axis: lax.axis_index(axis) for axis in ALL}
    row = place["z"] * SIDE + place["y"]
    col = place["x"] * CORES + place["core"]
    cells = far_right.shape[-1]
    all_members = log_state.shape[0]
    members = all_members // PARTS
    sides = far_left.shape[2]

    right = masked_right(far_right, ranks, jnp.stack([row, col]))
    right = lax.all_to_all(right, "y", split_axis=0, concat_axis=0, tiled=True)
    left = turned_left(far_left[0])
    columns = jnp.stack([rate_coef, state_coef, normal_stress, inv_length], axis=1)

    planes = jnp.stack([(place["z"] + dz) % SIDE for dz in OFFSETS])

    def gathered(slips):
        return [slips] + [from_z(slips, dz) for dz in OFFSETS[1:]]

    def sent(coef):
        coef = coef.reshape(coef.shape[0], -1, members)
        coef = lax.all_to_all(coef, ("y", "x", "core"), split_axis=0, concat_axis=0, tiled=True)
        return coef.reshape(-1, members)

    steps = 4
    flops = 2 * sides * cells * left.shape[1] * members
    scratch = [pltpu.VMEM((sides * cells, members), jnp.float32)]

    def start(part):
        here = slice(part * members, (part + 1) * members)
        old = jnp.swapaxes(tractions[:, here], 1, 2)
        state = jnp.swapaxes(log_state[here], 0, 1)
        slip_rates, speed = friction_slip(old, state, *[columns[:, k : k + 1] for k in range(3)])
        slips = jnp.concatenate(slip_rates, axis=0)
        state_rates = (jnp.exp(-state) - speed) * columns[:, 3:]
        middle_state = state + time_step * state_rates
        half_state = state + 0.5 * time_step * state_rates
        return slips, (old, middle_state, half_state, columns)

    def first_section(coef, rates_near, rest, after):
        rest = (rates_near, *rest)
        out_shape = (
            jax.ShapeDtypeStruct((2 * cells, members), jnp.bfloat16),
            jax.ShapeDtypeStruct((sides, cells, members), jnp.float32),
            jax.ShapeDtypeStruct((cells, members), jnp.float32),
        )
        return call(
            first_kernel, "first_section", (steps,),
            far_specs(coef, left, steps) + [whole(v) for v in rest] + [ANY] * len(after),
            [whole(v) for v in out_shape],
            out_shape, (coef, left, *rest, *after), flops, scratch,
        )

    def second_section(part, coef, slabs, half_tractions, before, after):
        rest = (*slabs, near_blocks[0], half_tractions)
        return call(
            second_kernel, "second_section", (steps,),
            far_specs(coef, left, steps) + [whole(v) for v in rest]
            + [ANY] * (len(before) + len(after)),
            pl.BlockSpec((sides, members, cells), lambda k: (0, part, 0)),
            jax.ShapeDtypeStruct((sides, all_members, cells), jnp.float32),
            (coef, left, *rest, *before, *after), flops, scratch,
            {7: 0} if before else None,
        )

    def neighbours(slips):
        return [beside(slips, -1), slips, beside(slips, 1)]

    begun = [start(part) for part in range(PARTS)]
    around = [gathered(slips) for slips, _ in begun]
    slabs = [neighbours(slips) for slips, _ in begun]
    before = (left, columns, *around[1], *[v[k] for v in slabs for k in (0, 2)])
    coefs = [coefficients_of(around[0], planes, right, before)]
    arrived = [sent(coefs[0])]
    coefs.append(coefficients_of(around[1], planes, right, (coefs[0],)))
    arrived.append(sent(coefs[1]))
    near_rates = [near_part(v, near_blocks[0], (coefs[1],)) for v in slabs]
    first, slabs = [], []
    for part in range(PARTS):
        first.append(first_section(arrived[part], near_rates[part], begun[part][1], (coefs[-1],)))
        slabs.append(neighbours(first[part][0]))
        early = slabs[0] if part == 0 else ()
        coefs.append(coefficients_of(gathered(first[part][0]), planes, right, early))
        arrived.append(sent(coefs[-1]))
    result = second_section(0, arrived[2], slabs[0], first[0][1], (), (coefs[3],))
    result = second_section(1, arrived[3], slabs[1], first[1][1], (result,), ())
    new_state = jnp.concatenate([jnp.swapaxes(v[2], 0, 1) for v in first], axis=0)
    return (result, new_state)


def solution(mesh):
    mesh = Mesh(mesh.devices.reshape(SIDE, SIDE, SIDE, CORES), ALL)
    row, col = ("z", "y"), ("x", "core")
    placed = (
        P(None, None, ALL),
        P(None, ALL),
        P(ALL),
        P(ALL),
        P(ALL),
        P(ALL),
        P(ALL, None, None, None, None, None),
        P(row, col, None, None, None),
        P(ALL, None, None, None, None),
        P(row, col),
    )
    return jax.shard_map(
        on_device,
        mesh=mesh,
        in_specs=placed,
        out_specs=(P(None, None, ALL), P(None, ALL)),
        check_vma=False,
    )
```
